32 devices in a mesh: ta: 4 (over z), xyz: 8 (over y, x, core).
Axes of the slice: x: 2, y: 2, z: 4, core: 2. Of those that a mesh axis runs over, the one named last changes fastest.
Arguments:
- residual: bfloat16 [512, 4608], P(('ta', 'xyz')), may hold values from -6 to 6
- iterate: bfloat16 [512, 4608], P(('ta', 'xyz')), may hold values from -6 to 6
- prolongator: bfloat16 [512, 12288], P(('ta', 'xyz')), may hold values from -0.3125 to 0.3125
- coarse_links: bfloat16 [9, 1024, 2048], P(None, ('ta', 'xyz')), may hold values from -0.125 to 0.125
- owner_counts: int32 [4, 8], P('ta'), may hold values from 1 to 32, 128 in all within a row
Outputs:
- corrected: bfloat16 [512, 4608], P(('ta', 'xyz'))
The draws below stay inside these ranges and needn't reach their ends.
Inputs may be any that keep to these rules, and one draw needn't show every extreme that they name: `owner_counts`: row t gives how many sites of time slice t each xyz index owns; each row sums to 128 and its largest entry is exactly 32.
All inputs are finite; a program needn't handle non-finite values.
Results may differ from the reference program's by a relative error of at most 0.0038.
Values may be sent and summed in bfloat16 or wider, within the bound.
A program may use at most 64 MiB of HBM per device.

```python
import math
import jax
import jax.numpy as jnp
import numpy as np
from jax import lax

NV = 32
FB = 192
RHS = 12
LY = 2
LZ = 8
SWEEPS = 2
CAP = 32
SLAB = 128
SITES = 512
TILES = 1024
N_TA = 4
N_XYZ = 8


def block_scale(key, dims, split, smallest, high):
    level = 1.0
    for position, blocks in split:
        draws = jax.random.uniform(jax.random.fold_in(jax.random.fold_in(key, 6), position), (blocks,), jnp.float32, smallest / len(split), high / len(split))
        level = level * jnp.repeat(jnp.exp(draws), dims[position] // blocks).reshape((-1,) + (1,) * (len(dims) - 1 - position))
    return level


def length_profile(count, total, bound, lean):
    portions = [(1 << 20) // math.isqrt(grade ** lean) + 1 for grade in range(2, count + 1)]
    spare, holding = total - bound - (count - 1), [1] * (count - 1)
    while spare > 0:
        candidates = [i for i in range(count - 1) if holding[i] < bound]
        whole, remaining = sum([portions[i] for i in candidates]), spare
        for i in candidates:
            more = min(bound - holding[i], max(1, remaining * portions[i] // whole), spare)
            holding[i] = holding[i] + more
            spare = spare - more
    return np.array([bound] + holding)


def ragged_sizes(rng, number_of, total, bound, skew):
    if number_of == 2:
        one = jax.random.randint(rng, (), max(1, total - bound), min(bound, total - 1) + 1)
        return jnp.stack([one, total - one])
    sizes = jnp.asarray(length_profile(number_of, total, bound, skew), jnp.int32)
    twos = (number_of - 1) // 2
    source_of, receiver = sizes[1:1 + 2 * twos:2], sizes[2:2 + 2 * twos:2]
    slack = jnp.minimum(source_of - 1, bound - receiver)
    shifted = jax.random.randint(jax.random.fold_in(rng, 1), (twos,), 0, 1 << 20) % (slack + 1)
    sizes = sizes.at[1:1 + 2 * twos:2].set(source_of - shifted).at[2:2 + 2 * twos:2].set(receiver + shifted)
    return sizes[jax.random.permutation(jax.random.fold_in(rng, 2), number_of)]


def scatter_about(own_key, extent, spread, most, shards=(), held_as=jnp.bfloat16):
    values = jax.random.normal(own_key, extent, jnp.float32) * spread
    if len(shards) > 0:
        values = block_scale(own_key, extent, shards, -0.22, 0.18) * values
    return jnp.clip(values, min=-most, max=most).astype(held_as)


def setup_inputs(seed: int = 0) -> dict:
    streams_of = jax.random.split(jax.random.key(seed), 6)
    residual = scatter_about(streams_of[0], (SITES, RHS * 2 * FB), 1.0, 6.0, ((0, 32),))
    iterate = scatter_about(streams_of[1], (SITES, RHS * 2 * FB), 1.0, 6.0, ((0, 32),))
    prolongator = scatter_about(streams_of[2], (SITES, 2 * NV * FB), (2 * FB) ** -0.5, 0.3125, ((0, 32),))
    coarse_links = scatter_about(streams_of[3], (9, TILES, 2 * NV * NV), (64 * NV) ** -0.5, 0.125, ((1, 32),))
    owner_counts = jax.vmap(lambda own: ragged_sizes(own, N_XYZ, SLAB, CAP, 2))(jax.random.split(streams_of[4], N_TA)).reshape((N_TA, N_XYZ)).astype(jnp.int32)
    return dict(residual=residual, iterate=iterate, prolongator=prolongator, coarse_links=coarse_links, owner_counts=owner_counts)


def restrict(fine_rows, basis_rows):
    count_rows = fine_rows.shape[0]
    vector = fine_rows.astype(jnp.float32).reshape(count_rows, RHS, 2, FB)
    matrix = basis_rows.astype(jnp.float32).reshape(count_rows, 2, NV, FB)
    real_part = jnp.einsum("bif,brf->bri", matrix[:, 0], vector[:, :, 0]) + jnp.einsum("bif,brf->bri", matrix[:, 1], vector[:, :, 1])
    imag_part = jnp.einsum("bif,brf->bri", matrix[:, 0], vector[:, :, 1]) - jnp.einsum("bif,brf->bri", matrix[:, 1], vector[:, :, 0])
    return jnp.stack([real_part, imag_part], axis=2).reshape(count_rows, RHS * 2 * NV).astype(jnp.bfloat16)


def prolong(coarse_rows, basis_rows):
    count_rows = coarse_rows.shape[0]
    vector = coarse_rows.astype(jnp.float32).reshape(count_rows, RHS, 2, NV)
    matrix = basis_rows.astype(jnp.float32).reshape(count_rows, 2, NV, FB)
    real_part = jnp.einsum("bif,bri->brf", matrix[:, 0], vector[:, :, 0]) - jnp.einsum("bif,bri->brf", matrix[:, 1], vector[:, :, 1])
    imag_part = jnp.einsum("bif,bri->brf", matrix[:, 0], vector[:, :, 1]) + jnp.einsum("bif,bri->brf", matrix[:, 1], vector[:, :, 0])
    return jnp.stack([real_part, imag_part], axis=2).reshape(count_rows, RHS * 2 * FB)


def hopping(link_rows, neighbours):
    count_rows = neighbours.shape[1]
    matrix = link_rows.astype(jnp.float32).reshape(9, count_rows, 2, NV, NV)
    vector = neighbours.astype(jnp.float32).reshape(9, count_rows, RHS, 2, NV)
    real_part = jnp.einsum("msij,msrj->sri", matrix[:, :, 0], vector[:, :, :, 0]) - jnp.einsum("msij,msrj->sri", matrix[:, :, 1], vector[:, :, :, 1])
    imag_part = jnp.einsum("msij,msrj->sri", matrix[:, :, 0], vector[:, :, :, 1]) + jnp.einsum("msij,msrj->sri", matrix[:, :, 1], vector[:, :, :, 0])
    return jnp.stack([real_part, imag_part], axis=2).reshape(count_rows, RHS * 2 * NV)


def spatial_neighbours(positions, slab_rows):
    extent_x = slab_rows // (LY * LZ)
    coord_x = positions % extent_x
    coord_z = (positions // extent_x) % LZ
    coord_y = positions // (extent_x * LZ)

    def site_of(along_x, along_y, along_z):
        return (((along_y % LY) * LZ + along_z % LZ) * extent_x + along_x % extent_x).astype(jnp.int32)

    return [site_of(coord_x + 1, coord_y, coord_z), site_of(coord_x - 1, coord_y, coord_z),
            site_of(coord_x, coord_y + 1, coord_z), site_of(coord_x, coord_y - 1, coord_z),
            site_of(coord_x, coord_y, coord_z + 1), site_of(coord_x, coord_y, coord_z - 1)]


def tile_source(positions, run_starts, run_ends, capacity):
    owners = jnp.sum((run_ends[None, :] <= positions[:, None]).astype(jnp.int32), axis=1)
    ranks = jnp.arange(run_ends.shape[0], dtype=jnp.int32)
    begin = jnp.sum(jnp.where(ranks[None, :] == owners[:, None], run_starts[None, :], 0), axis=1).astype(jnp.int32)
    return (owners * capacity + positions - begin).astype(jnp.int32)


def reference(residual, iterate, prolongator, coarse_links, owner_counts):
    fine_slices = residual.reshape(N_TA, SLAB, RHS * 2 * FB)
    basis_slices = prolongator.reshape(N_TA, SLAB, 2 * NV * FB)
    coarse_rhs = lax.map(lambda pair: restrict(pair[0], pair[1]), (fine_slices, basis_slices))
    positions = jnp.arange(SLAB, dtype=jnp.int32)
    spatial_rows = spatial_neighbours(positions, SLAB)

    def sweep_slice(time_index, current):
        counts_row = owner_counts[time_index]
        run_ends = jnp.cumsum(counts_row).astype(jnp.int32)
        run_starts = (run_ends - counts_row).astype(jnp.int32)
        source = tile_source(positions, run_starts, run_ends, CAP)
        block = lax.dynamic_slice_in_dim(coarse_links, (time_index * N_XYZ * CAP).astype(jnp.int32), N_XYZ * CAP, 1)
        link_rows = jnp.take(block, source, axis=1)
        here = current[time_index]
        after = current[(time_index + 1) % N_TA]
        before = current[(time_index - 1 + N_TA) % N_TA]
        row_list = [here] + [jnp.take(here, rows, axis=0) for rows in spatial_rows] + [after, before]
        neighbours = jnp.stack(row_list)
        updated = coarse_rhs[time_index].astype(jnp.float32) - hopping(link_rows, neighbours)
        return updated.astype(jnp.bfloat16)

    current = coarse_rhs
    for sweep_index in range(SWEEPS):
        current = lax.map(lambda time_index, state=current: sweep_slice(time_index, state), jnp.arange(N_TA, dtype=jnp.int32))
    iterate_slices = iterate.reshape(N_TA, SLAB, RHS * 2 * FB)

    def finish(triple):
        return (triple[0].astype(jnp.float32) + prolong(triple[1], triple[2])).astype(jnp.bfloat16)

    corrected = lax.map(finish, (iterate_slices, current, basis_slices))
    return corrected.reshape(SITES, RHS * 2 * FB)
```

```python
import functools

import jax
import jax.numpy as jnp
from jax import lax
from jax.experimental import pallas as pl
from jax.experimental.pallas import tpu as pltpu
from jax.sharding import PartitionSpec as P

NV = 32
FB = 192
RHS = 12
LY = 2
LZ = 8
SWEEPS = 2
COLS = RHS * 2 * NV
LANES = 128
UNITS = COLS // LANES
GROUP = 16
MESH = pl.DeviceIdType.MESH
F32 = jnp.float32
BF16 = jnp.bfloat16


def basis_block(basis_rows):
    count_rows = basis_rows.shape[0]
    matrix = basis_rows.reshape(count_rows, 2, NV, FB)
    real_rows = jnp.concatenate([matrix[:, 0], matrix[:, 1]], axis=2)
    imag_rows = jnp.concatenate([-matrix[:, 1], matrix[:, 0]], axis=2)
    return jnp.concatenate([real_rows, imag_rows], axis=1)


def restrict(fine_rows, block):
    count_rows = fine_rows.shape[0]
    vector = fine_rows.reshape(count_rows, RHS, 2 * FB)
    result = jnp.einsum("bkf,brf->brk", block, vector, preferred_element_type=F32)
    return result.reshape(count_rows, COLS).astype(BF16)


def prolong(coarse_rows, block):
    count_rows = coarse_rows.shape[0]
    vector = coarse_rows.reshape(count_rows, RHS, 2 * NV)
    result = jnp.einsum("bkf,brk->brf", block, vector, preferred_element_type=F32)
    return result.reshape(count_rows, RHS * 2 * FB)


def iota(shape, dim):
    return lax.broadcasted_iota(jnp.int32, shape, dim)


def dot(left, right):
    return jnp.dot(left, right, preferred_element_type=F32)


def dot_nt(left, right):
    return lax.dot_general(left, right, (((1,), (1,)), ((), ())), preferred_element_type=F32)


def one_hot(condition):
    return jnp.where(condition, 1.0, 0.0).astype(BF16)


def shifted_sites(site, extent_x):
    bits_x = extent_x.bit_length() - 1
    x = site & (extent_x - 1)
    z = (site >> bits_x) & (LZ - 1)
    y = site >> (bits_x + 3)

    def site_of(ax, ay, az):
        return ((((ay & (LY - 1)) << 3) + (az & (LZ - 1))) << bits_x) + (ax & (extent_x - 1))

    return [
        site,
        site_of(x - 1, y, z),
        site_of(x + 1, y, z),
        site_of(x, y - 1, z),
        site_of(x, y + 1, z),
        site_of(x, y, z - 1),
        site_of(x, y, z + 1),
    ]


def coarse_kernel(
    n_ta, n_xyz, cap, block,
    rhs_ref, counts_ref, links_hbm, own_ref,
    vec, tiles, fin, scat, zin, zout, cnt, links, weights, lhs, part, perm, pick,
    send_a, recv_a, send_c, recv_c, send_e, recv_e, send_z, recv_z, send_n, recv_n, sem_l,
):
    slab = n_xyz * block
    extent_x = slab // (LY * LZ)
    t = lax.axis_index("ta")
    o = lax.axis_index("xyz")
    up = lax.rem(t + 1, n_ta)
    down = lax.rem(t + n_ta - 1, n_ta)
    peers = [lax.rem(o + d, n_xyz) for d in range(1, n_xyz)]

    load = pltpu.make_async_copy(links_hbm, links, sem_l)
    load.start()
    barrier = pltpu.get_barrier_semaphore()
    for peer in peers:
        pl.semaphore_signal(barrier, inc=1, device_id=(t, peer), device_id_type=MESH)
    for row in (up, down):
        pl.semaphore_signal(barrier, inc=1, device_id=(row, o), device_id_type=MESH)

    cnt[0] = jnp.zeros((8, LANES), jnp.int32)
    cnt[0, 0:1, 0:n_xyz] = counts_ref[...]
    mine = pl.ds(pl.multiple_of(o * block, block), block)
    my_tile = pl.ds(pl.multiple_of(o * cap, cap), cap)
    vec[mine, :] = rhs_ref[...]
    pl.semaphore_wait(barrier, n_xyz + 1)

    def remote(src, dst, send, recv, device):
        copy = pltpu.make_async_remote_copy(
            src_ref=src, dst_ref=dst, send_sem=send, recv_sem=recv,
            device_id=device, device_id_type=MESH,
        )
        copy.start()
        return copy

    def to_slice(src_of, dst, send, recv):
        return [
            remote(src_of(peer), dst, send.at[d], recv.at[d], (t, peer))
            for d, peer in enumerate(peers)
        ]

    copies_n = [
        remote(cnt.at[0], cnt.at[1 + side], send_n.at[side], recv_n.at[side], (row, o))
        for side, row in enumerate((down, up))
    ]
    copies_a = to_slice(lambda peer: vec.at[mine], vec.at[mine], send_a, recv_a)

    r_id, c_id = iota((512, 512), 0), iota((512, 512), 1)
    perm[...] = one_hot(c_id == ((r_id >> 5) & 3) * 128 + (r_id >> 7) * 32 + (r_id & 31))
    pick[...] = one_hot((iota((2048, LANES), 0) >> 4) == iota((2048, LANES), 1))

    counts = cnt[0, 0:1, :].astype(F32)
    lane = iota((1, LANES), 1)

    def start_of(row):
        return jnp.sum(jnp.where(lane < o, row, 0.0), axis=1, keepdims=True).astype(jnp.int32)

    start = start_of(counts)
    own_count = jnp.sum(jnp.where(lane == o, counts, 0.0), axis=1, keepdims=True).astype(jnp.int32)
    position = start + iota((cap, slab), 0)
    gather = jnp.concatenate(
        [one_hot(position == site) for site in shifted_sites(iota((cap, slab), 1), extent_x)], axis=0
    )
    slot_owner = iota((1, n_xyz * cap), 1) // cap
    slot_start = jnp.zeros((1, n_xyz * cap), jnp.int32)
    slot_count = jnp.zeros((1, n_xyz * cap), jnp.int32)
    for p in range(n_xyz):
        value = cnt[0, 0:1, p:p + 1]
        slot_start = slot_start + jnp.where(slot_owner > p, value, 0)
        slot_count = slot_count + jnp.where(slot_owner == p, value, 0)
    slot = iota((1, n_xyz * cap), 1) - slot_owner * cap
    slot_site = jnp.where(slot < slot_count, slot_start + slot, -1)
    held = one_hot(iota((slab, n_xyz * cap), 0) == slot_site)
    gather_tiles = dot(gather, held).astype(BF16)
    slot_lane = iota((slab, cap), 1)
    spread = one_hot((iota((slab, cap), 0) == start + slot_lane) & (slot_lane < own_count))

    load.wait()
    lane_q = iota((cap, LANES), 1)

    def minus_identity(q):
        place = lane_q + q * LANES
        return jnp.where((place >> 5) == (place & 31), -1.0, 0.0).astype(BF16)

    for group in range(3):
        rows = []
        for q in range(16):
            part_q = slice(q * LANES, (q + 1) * LANES)
            if group == 0:
                pieces = [links[m, :, part_q] for m in (0, 1, 2, 3)]
            elif group == 1:
                pieces = [links[m, :, part_q] for m in (4, 5, 6)] + [minus_identity(q)]
            else:
                pieces = [links[m, :, part_q] for m in (7, 8)]
            rows.append(jnp.concatenate(pieces, axis=1))
        stacked = jnp.concatenate(rows, axis=0)
        moved = dot(stacked, perm[0:stacked.shape[1], :]).astype(BF16)
        for q in range(16):
            for a in range(4):
                for g in range(2):
                    at = (q * 4 + a) * GROUP
                    first = q * cap + g * GROUP
                    weights[g, at:at + GROUP, group * LANES:(group + 1) * LANES] = moved[
                        first:first + GROUP, a * LANES:(a + 1) * LANES]

    def set_lhs(group, blocks):
        stacked = jnp.concatenate(
            [jnp.concatenate([b[:, u * LANES:(u + 1) * LANES] for b in blocks], axis=1) for u in range(UNITS)],
            axis=0,
        )
        moved = dot(stacked, perm[0:stacked.shape[1], :]).astype(BF16)
        for u in range(UNITS):
            for b in range(4):
                for g in range(2):
                    at = (u * 4 + b) * GROUP
                    first = u * cap + g * GROUP
                    lhs[g, at:at + GROUP, group * LANES:(group + 1) * LANES] = moved[
                        first:first + GROUP, b * LANES:(b + 1) * LANES]

    for copy in copies_n:
        copy.wait()
    away = []
    for side in range(2):
        row_start = start_of(cnt[1 + side, 0:1, :].astype(F32))
        away.append(one_hot(row_start + iota((cap, slab), 0) == iota((cap, slab), 1)))
    away = jnp.concatenate(away, axis=0)
    away_tiles = dot(away, held).astype(BF16)

    rhs_rows = None
    diagonal = (iota((GROUP, 512), 1) & (GROUP - 1)) == iota((GROUP, 512), 0)
    for sweep in range(SWEEPS):
        if sweep == 0:
            for copy in copies_a:
                copy.wait()
            source, near, far = vec, gather, away
        else:
            for copy in copies_c:
                copy.wait()
            source, near, far = tiles, gather_tiles, away_tiles
        full = source[...]
        zout[sweep] = dot(far, full).astype(BF16)
        copies_z = [
            remote(
                zout.at[sweep, pl.ds(side * cap, cap)], zin.at[sweep, pl.ds((1 - side) * cap, cap)],
                send_z.at[sweep, side], recv_z.at[sweep, side], (row, o),
            )
            for side, row in enumerate((up, down))
        ]
        around = dot(near, full).astype(BF16)
        blocks = [around[m * cap:(m + 1) * cap] for m in range(7)]
        if sweep == 0:
            rhs_rows = blocks[0]
        set_lhs(0, blocks[0:4])
        set_lhs(1, blocks[4:7] + [rhs_rows])
        for g in range(2):
            part[g] = dot_nt(lhs[g, :, 0:256], weights[g, :, 0:256])
        for copy in copies_z:
            copy.wait()
        set_lhs(2, [zin[sweep, 0:cap], zin[sweep, cap:2 * cap]])
        updated = []
        for g in range(2):
            total = part[g] + dot_nt(lhs[g, :, 256:384], weights[g, :, 256:384])
            rows = []
            for u in range(UNITS):
                pieces = []
                for r in range(2):
                    at = (u * 4 + r * 2) * GROUP
                    from_real, from_imag = total[at:at + GROUP], total[at + GROUP:at + 2 * GROUP]
                    real = from_imag[:, 512:] - from_real[:, :512]
                    imag = -(from_real[:, 512:] + from_imag[:, :512])
                    pieces += [jnp.where(diagonal, v, 0.0).astype(BF16) for v in (real, imag)]
                rows.append(jnp.concatenate(pieces, axis=1))
            picked = dot(jnp.concatenate(rows, axis=0), pick[...]).astype(BF16)
            updated.append(jnp.concatenate([picked[u * GROUP:(u + 1) * GROUP] for u in range(UNITS)], axis=1))
        tile = jnp.concatenate(updated, axis=0)
        if sweep < SWEEPS - 1:
            tiles[my_tile, :] = tile
            copies_c = to_slice(lambda peer: tiles.at[my_tile], tiles.at[my_tile], send_c, recv_c)
    scat[...] = dot(spread, tile).astype(BF16)
    copies_e = to_slice(
        lambda peer: scat.at[pl.ds(pl.multiple_of(peer * block, block), block)], fin.at[o], send_e, recv_e
    )
    fin[o] = scat[mine, :]
    for copy in copies_e:
        copy.wait()
    total = fin[0].astype(F32)
    for p in range(1, n_xyz):
        total = total + fin[p].astype(F32)
    own_ref[...] = total.astype(BF16)


def on_device(n_ta, n_xyz, residual, iterate, prolongator, coarse_links, owner_counts):
    block = residual.shape[0]
    cap = coarse_links.shape[1]
    slab = n_xyz * block
    basis_real = basis_block(prolongator)
    coarse_rhs = restrict(residual, basis_real)
    vmem = pl.BlockSpec(memory_space=pltpu.VMEM)
    dma = pltpu.SemaphoreType.DMA
    own_piece = pl.pallas_call(
        functools.partial(coarse_kernel, n_ta, n_xyz, cap, block),
        out_shape=jax.ShapeDtypeStruct((block, COLS), BF16),
        in_specs=[vmem, vmem, pl.BlockSpec(memory_space=pl.ANY)],
        out_specs=vmem,
        scratch_shapes=[
            pltpu.VMEM((slab, COLS), BF16),
            pltpu.VMEM((n_xyz * cap, COLS), BF16),
            pltpu.VMEM((n_xyz, block, COLS), BF16),
            pltpu.VMEM((slab, COLS), BF16),
            pltpu.VMEM((SWEEPS, 2 * cap, COLS), BF16),
            pltpu.VMEM((SWEEPS, 2 * cap, COLS), BF16),
            pltpu.VMEM((3, 8, LANES), jnp.int32),
            pltpu.VMEM(coarse_links.shape, BF16),
            pltpu.VMEM((2, 64 * GROUP, 3 * LANES), BF16),
            pltpu.VMEM((2, 24 * GROUP, 3 * LANES), BF16),
            pltpu.VMEM((2, 24 * GROUP, 64 * GROUP), F32),
            pltpu.VMEM((512, 512), BF16),
            pltpu.VMEM((2048, LANES), BF16),
            dma((n_xyz - 1,)), dma((n_xyz - 1,)),
            dma((n_xyz - 1,)), dma((n_xyz - 1,)),
            dma((n_xyz - 1,)), dma((n_xyz - 1,)),
            dma((SWEEPS, 2)), dma((SWEEPS, 2)),
            dma((2,)), dma((2,)),
            dma,
        ],
        compiler_params=pltpu.CompilerParams(
            collective_id=0, has_side_effects=True, vmem_limit_bytes=48 * 1024 * 1024
        ),
    )(coarse_rhs, owner_counts, coarse_links)
    correction = prolong(own_piece, basis_real)
    return (iterate.astype(F32) + correction).astype(BF16)


def solution(mesh):
    in_specs = (
        P(("ta", "xyz"), None),
        P(("ta", "xyz"), None),
        P(("ta", "xyz"), None),
        P(None, ("ta", "xyz"), None),
        P("ta", None),
    )
    out_specs = P(("ta", "xyz"), None)
    return jax.shard_map(
        functools.partial(on_device, mesh.shape["ta"], mesh.shape["xyz"]),
        mesh=mesh, in_specs=in_specs, out_specs=out_specs, check_vma=False,
    )
```

```python
import functools

import jax
import jax.numpy as jnp
from jax import lax
from jax.experimental import pallas as pl
from jax.experimental.pallas import tpu as pltpu
from jax.sharding import PartitionSpec as P

NV = 32
FB = 192
RHS = 12
LY = 2
LZ = 8
SWEEPS = 2
COLS = RHS * 2 * NV
LANES = 128
UNITS = COLS // LANES
GROUP = 16
MESH = pl.DeviceIdType.MESH
F32 = jnp.float32
BF16 = jnp.bfloat16


def basis_block(basis_rows):
    count_rows = basis_rows.shape[0]
    matrix = basis_rows.reshape(count_rows, 2, NV, FB)
    real_rows = jnp.concatenate([matrix[:, 0], matrix[:, 1]], axis=2)
    imag_rows = jnp.concatenate([-matrix[:, 1], matrix[:, 0]], axis=2)
    return jnp.concatenate([real_rows, imag_rows], axis=1)


def restrict(fine_rows, block):
    count_rows = fine_rows.shape[0]
    vector = fine_rows.reshape(count_rows, RHS, 2 * FB)
    result = jnp.einsum("bkf,brf->brk", block, vector, preferred_element_type=F32)
    return result.reshape(count_rows, COLS).astype(BF16)


def prolong(coarse_rows, block):
    count_rows = coarse_rows.shape[0]
    vector = coarse_rows.reshape(count_rows, RHS, 2 * NV)
    result = jnp.einsum("bkf,brk->brf", block, vector, preferred_element_type=F32)
    return result.reshape(count_rows, RHS * 2 * FB)


def iota(shape, dim):
    return lax.broadcasted_iota(jnp.int32, shape, dim)


def dot(left, right):
    return jnp.dot(left, right, preferred_element_type=F32)


def dot_nt(left, right):
    return lax.dot_general(left, right, (((1,), (1,)), ((), ())), preferred_element_type=F32)


def one_hot(condition):
    return jnp.where(condition, 1.0, 0.0).astype(BF16)


def shifted_sites(site, extent_x):
    bits_x = extent_x.bit_length() - 1
    x = site & (extent_x - 1)
    z = (site >> bits_x) & (LZ - 1)
    y = site >> (bits_x + 3)

    def site_of(ax, ay, az):
        return ((((ay & (LY - 1)) << 3) + (az & (LZ - 1))) << bits_x) + (ax & (extent_x - 1))

    return [
        site,
        site_of(x - 1, y, z),
        site_of(x + 1, y, z),
        site_of(x, y - 1, z),
        site_of(x, y + 1, z),
        site_of(x, y, z - 1),
        site_of(x, y, z + 1),
    ]


def coarse_kernel(
    n_ta, n_xyz, cap, block,
    rhs_ref, counts_ref, links_hbm, own_ref,
    vec, tiles, fin, scat, zin, zout, beside, cnt, links, weights, lhs, part, perm, pick,
    send_a, recv_a, send_c, recv_c, send_e, recv_e, send_z, recv_z, send_b, recv_b, send_n, recv_n, sem_l,
):
    slab = n_xyz * block
    extent_x = slab // (LY * LZ)
    t = lax.axis_index("ta")
    o = lax.axis_index("xyz")
    up = lax.rem(t + 1, n_ta)
    down = lax.rem(t + n_ta - 1, n_ta)
    peers = [lax.rem(o + d, n_xyz) for d in range(1, n_xyz)]

    load = pltpu.make_async_copy(links_hbm, links, sem_l)
    load.start()
    barrier = pltpu.get_barrier_semaphore()
    for peer in peers:
        pl.semaphore_signal(barrier, inc=1, device_id=(t, peer), device_id_type=MESH)
    for row in (up, down):
        for peer in [o] + peers:
            pl.semaphore_signal(barrier, inc=1, device_id=(row, peer), device_id_type=MESH)

    cnt[0] = jnp.zeros((8, LANES), jnp.int32)
    cnt[0, 0:1, 0:n_xyz] = counts_ref[...]
    mine = pl.ds(pl.multiple_of(o * block, block), block)
    my_tile = pl.ds(pl.multiple_of(o * cap, cap), cap)
    vec[mine, :] = rhs_ref[...]
    pl.semaphore_wait(barrier, 3 * n_xyz - 1)

    def remote(src, dst, send, recv, device):
        copy = pltpu.make_async_remote_copy(
            src_ref=src, dst_ref=dst, send_sem=send, recv_sem=recv,
            device_id=device, device_id_type=MESH,
        )
        copy.start()
        return copy

    def to_slice(src_of, dst, send, recv):
        return [
            remote(src_of(peer), dst, send.at[d], recv.at[d], (t, peer))
            for d, peer in enumerate(peers)
        ]

    copies_n = [
        remote(cnt.at[0], cnt.at[1 + side], send_n.at[side], recv_n.at[side], (row, o))
        for side, row in enumerate((down, up))
    ]
    copies_a = to_slice(lambda peer: vec.at[mine], vec.at[mine], send_a, recv_a)
    copies_b = [
        remote(vec.at[mine], beside.at[1 - side, mine], send_b.at[side, d], recv_b.at[side, d], (row, peer))
        for d, peer in enumerate([o] + peers)
        for side, row in enumerate((up, down))
    ]

    r_id, c_id = iota((512, 512), 0), iota((512, 512), 1)
    perm[...] = one_hot(c_id == ((r_id >> 5) & 3) * 128 + (r_id >> 7) * 32 + (r_id & 31))
    pick[...] = one_hot((iota((2048, LANES), 0) >> 4) == iota((2048, LANES), 1))

    counts = cnt[0, 0:1, :].astype(F32)
    lane = iota((1, LANES), 1)

    def start_of(row):
        return jnp.sum(jnp.where(lane < o, row, 0.0), axis=1, keepdims=True).astype(jnp.int32)

    start = start_of(counts)
    own_count = jnp.sum(jnp.where(lane == o, counts, 0.0), axis=1, keepdims=True).astype(jnp.int32)
    position = start + iota((cap, slab), 0)
    gather = jnp.concatenate(
        [one_hot(position == site) for site in shifted_sites(iota((cap, slab), 1), extent_x)], axis=0
    )
    slot_owner = iota((1, n_xyz * cap), 1) // cap
    slot_start = jnp.zeros((1, n_xyz * cap), jnp.int32)
    slot_count = jnp.zeros((1, n_xyz * cap), jnp.int32)
    for p in range(n_xyz):
        value = cnt[0, 0:1, p:p + 1]
        slot_start = slot_start + jnp.where(slot_owner > p, value, 0)
        slot_count = slot_count + jnp.where(slot_owner == p, value, 0)
    slot = iota((1, n_xyz * cap), 1) - slot_owner * cap
    slot_site = jnp.where(slot < slot_count, slot_start + slot, -1)
    held = one_hot(iota((slab, n_xyz * cap), 0) == slot_site)
    gather_tiles = dot(gather, held).astype(BF16)
    slot_lane = iota((slab, cap), 1)
    spread = one_hot((iota((slab, cap), 0) == start + slot_lane) & (slot_lane < own_count))

    load.wait()
    lane_q = iota((cap, LANES), 1)

    def minus_identity(q):
        place = lane_q + q * LANES
        return jnp.where((place >> 5) == (place & 31), -1.0, 0.0).astype(BF16)

    for group in range(3):
        rows = []
        for q in range(16):
            part_q = slice(q * LANES, (q + 1) * LANES)
            if group == 0:
                pieces = [links[m, :, part_q] for m in (0, 1, 2, 3)]
            elif group == 1:
                pieces = [links[m, :, part_q] for m in (4, 5, 6)] + [minus_identity(q)]
            else:
                pieces = [links[m, :, part_q] for m in (7, 8)]
            rows.append(jnp.concatenate(pieces, axis=1))
        stacked = jnp.concatenate(rows, axis=0)
        moved = dot(stacked, perm[0:stacked.shape[1], :]).astype(BF16)
        for q in range(16):
            for a in range(4):
                for g in range(2):
                    at = (q * 4 + a) * GROUP
                    first = q * cap + g * GROUP
                    weights[g, at:at + GROUP, group * LANES:(group + 1) * LANES] = moved[
                        first:first + GROUP, a * LANES:(a + 1) * LANES]

    def set_lhs(group, blocks):
        stacked = jnp.concatenate(
            [jnp.concatenate([b[:, u * LANES:(u + 1) * LANES] for b in blocks], axis=1) for u in range(UNITS)],
            axis=0,
        )
        moved = dot(stacked, perm[0:stacked.shape[1], :]).astype(BF16)
        for u in range(UNITS):
            for b in range(4):
                for g in range(2):
                    at = (u * 4 + b) * GROUP
                    first = u * cap + g * GROUP
                    lhs[g, at:at + GROUP, group * LANES:(group + 1) * LANES] = moved[
                        first:first + GROUP, b * LANES:(b + 1) * LANES]

    rhs_rows = None
    diagonal = (iota((GROUP, 512), 1) & (GROUP - 1)) == iota((GROUP, 512), 0)
    for sweep in range(SWEEPS):
        if sweep == 0:
            for copy in copies_a:
                copy.wait()
            source, near = vec, gather
        else:
            for copy in copies_c:
                copy.wait()
            source, near = tiles, gather_tiles
        full = source[...]
        if sweep > 0:
            zout[...] = dot(away_tiles, full).astype(BF16)
            copies_z = [
                remote(
                    zout.at[pl.ds(side * cap, cap)], zin.at[pl.ds((1 - side) * cap, cap)],
                    send_z.at[side], recv_z.at[side], (row, o),
                )
                for side, row in enumerate((up, down))
            ]
        around = dot(near, full).astype(BF16)
        blocks = [around[m * cap:(m + 1) * cap] for m in range(7)]
        if sweep == 0:
            rhs_rows = blocks[0]
        set_lhs(0, blocks[0:4])
        set_lhs(1, blocks[4:7] + [rhs_rows])
        for g in range(2):
            part[g] = dot_nt(lhs[g, :, 0:256], weights[g, :, 0:256])
        if sweep == 0:
            for copy in copies_b:
                copy.wait()
            set_lhs(2, [dot(gather[0:cap], beside[side]).astype(BF16) for side in range(2)])
        else:
            for copy in copies_z:
                copy.wait()
            set_lhs(2, [zin[0:cap], zin[cap:2 * cap]])
        updated = []
        for g in range(2):
            total = part[g] + dot_nt(lhs[g, :, 256:384], weights[g, :, 256:384])
            rows = []
            for u in range(UNITS):
                pieces = []
                for r in range(2):
                    at = (u * 4 + r * 2) * GROUP
                    from_real, from_imag = total[at:at + GROUP], total[at + GROUP:at + 2 * GROUP]
                    real = from_imag[:, 512:] - from_real[:, :512]
                    imag = -(from_real[:, 512:] + from_imag[:, :512])
                    pieces += [jnp.where(diagonal, v, 0.0).astype(BF16) for v in (real, imag)]
                rows.append(jnp.concatenate(pieces, axis=1))
            picked = dot(jnp.concatenate(rows, axis=0), pick[...]).astype(BF16)
            updated.append(jnp.concatenate([picked[u * GROUP:(u + 1) * GROUP] for u in range(UNITS)], axis=1))
        tile = jnp.concatenate(updated, axis=0)
        if sweep < SWEEPS - 1:
            tiles[my_tile, :] = tile
            copies_c = to_slice(lambda peer: tiles.at[my_tile], tiles.at[my_tile], send_c, recv_c)
            for copy in copies_n:
                copy.wait()
            away = []
            for side in range(2):
                row_start = start_of(cnt[1 + side, 0:1, :].astype(F32))
                away.append(one_hot(row_start + iota((cap, slab), 0) == iota((cap, slab), 1)))
            away = jnp.concatenate(away, axis=0)
            away_tiles = dot(away, held).astype(BF16)
    scat[...] = dot(spread, tile).astype(BF16)
    copies_e = to_slice(
        lambda peer: scat.at[pl.ds(pl.multiple_of(peer * block, block), block)], fin.at[o], send_e, recv_e
    )
    fin[o] = scat[mine, :]
    for copy in copies_e:
        copy.wait()
    total = fin[0].astype(F32)
    for p in range(1, n_xyz):
        total = total + fin[p].astype(F32)
    own_ref[...] = total.astype(BF16)


def on_device(n_ta, n_xyz, residual, iterate, prolongator, coarse_links, owner_counts):
    block = residual.shape[0]
    cap = coarse_links.shape[1]
    slab = n_xyz * block
    basis_real = basis_block(prolongator)
    coarse_rhs = restrict(residual, basis_real)
    vmem = pl.BlockSpec(memory_space=pltpu.VMEM)
    dma = pltpu.SemaphoreType.DMA
    own_piece = pl.pallas_call(
        functools.partial(coarse_kernel, n_ta, n_xyz, cap, block),
        out_shape=jax.ShapeDtypeStruct((block, COLS), BF16),
        in_specs=[vmem, vmem, pl.BlockSpec(memory_space=pl.ANY)],
        out_specs=vmem,
        scratch_shapes=[
            pltpu.VMEM((slab, COLS), BF16),
            pltpu.VMEM((n_xyz * cap, COLS), BF16),
            pltpu.VMEM((n_xyz, block, COLS), BF16),
            pltpu.VMEM((slab, COLS), BF16),
            pltpu.VMEM((2 * cap, COLS), BF16),
            pltpu.VMEM((2 * cap, COLS), BF16),
            pltpu.VMEM((2, slab, COLS), BF16),
            pltpu.VMEM((3, 8, LANES), jnp.int32),
            pltpu.VMEM(coarse_links.shape, BF16),
            pltpu.VMEM((2, 64 * GROUP, 3 * LANES), BF16),
            pltpu.VMEM((2, 24 * GROUP, 3 * LANES), BF16),
            pltpu.VMEM((2, 24 * GROUP, 64 * GROUP), F32),
            pltpu.VMEM((512, 512), BF16),
            pltpu.VMEM((2048, LANES), BF16),
            dma((n_xyz - 1,)), dma((n_xyz - 1,)),
            dma((n_xyz - 1,)), dma((n_xyz - 1,)),
            dma((n_xyz - 1,)), dma((n_xyz - 1,)),
            dma((2,)), dma((2,)),
            dma((2, n_xyz)), dma((2, n_xyz)),
            dma((2,)), dma((2,)),
            dma,
        ],
        compiler_params=pltpu.CompilerParams(
            collective_id=0, has_side_effects=True, vmem_limit_bytes=60 * 1024 * 1024
        ),
    )(coarse_rhs, owner_counts, coarse_links)
    correction = prolong(own_piece, basis_real)
    return (iterate.astype(F32) + correction).astype(BF16)


def solution(mesh):
    in_specs = (
        P(("ta", "xyz"), None),
        P(("ta", "xyz"), None),
        P(("ta", "xyz"), None),
        P(None, ("ta", "xyz"), None),
        P("ta", None),
    )
    out_specs = P(("ta", "xyz"), None)
    return jax.shard_map(
        functools.partial(on_device, mesh.shape["ta"], mesh.shape["xyz"]),
        mesh=mesh, in_specs=in_specs, out_specs=out_specs, check_vma=False,
    )
```

```python
import functools

import jax
import jax.numpy as jnp
from jax import lax
from jax.experimental import pallas as pl
from jax.experimental.pallas import tpu as pltpu
from jax.sharding import PartitionSpec as P

NV = 32
FB = 192
RHS = 12
LY = 2
LZ = 8
SWEEPS = 2
COLS = RHS * 2 * NV
LANES = 128
UNITS = COLS // LANES
GROUP = 16
MESH = pl.DeviceIdType.MESH
F32 = jnp.float32
BF16 = jnp.bfloat16


def iota(shape, dim):
    return lax.broadcasted_iota(jnp.int32, shape, dim)


def dot(left, right):
    return jnp.dot(left, right, preferred_element_type=F32)


def dot_nt(left, right):
    return lax.dot_general(left, right, (((1,), (1,)), ((), ())), preferred_element_type=F32)


def one_hot(condition):
    return jnp.where(condition, 1.0, 0.0).astype(BF16)


def shifted_sites(site, extent_x):
    bits_x = extent_x.bit_length() - 1
    x = site & (extent_x - 1)
    z = (site >> bits_x) & (LZ - 1)
    y = site >> (bits_x + 3)

    def site_of(ax, ay, az):
        return ((((ay & (LY - 1)) << 3) + (az & (LZ - 1))) << bits_x) + (ax & (extent_x - 1))

    return [
        site,
        site_of(x - 1, y, z),
        site_of(x + 1, y, z),
        site_of(x, y - 1, z),
        site_of(x, y + 1, z),
        site_of(x, y, z - 1),
        site_of(x, y, z + 1),
    ]


def on_diagonal(shape):
    return (iota(shape, 1) & (GROUP - 1)) == (iota(shape, 0) & (GROUP - 1))


def restrict(residual, basis, basis_rows, spots):
    wide = 2 * LANES
    lane = iota((GROUP, wide), 1)
    for h in range(2):
        for pair in range(NV):
            first = pair * 2 * FB + h * LANES
            basis_rows[h, pair * GROUP:(pair + 1) * GROUP, :] = basis[:, first:first + wide]
    real, imag = [], []
    for r in range(RHS):
        first = r * 2 * FB
        real.append(jnp.where(lane < FB, residual[:, first:first + wide], 0.0).astype(BF16))
        imag.append(jnp.where(lane >= wide - FB, residual[:, first + LANES:first + LANES + wide], 0.0).astype(BF16))
    real, imag = jnp.concatenate(real, axis=0), jnp.concatenate(imag, axis=0)
    row_id, col_id = iota((wide, wide), 0), iota((wide, wide), 1)
    real_late = dot(real, one_hot(col_id == row_id + 64)).astype(BF16)
    imag_early = dot(imag, one_hot(col_id == row_id - 64)).astype(BF16)
    lines = RHS * GROUP
    keep = on_diagonal((lines, wide))
    pieces = {}
    for h, pair in enumerate(((real, imag_early), (real_late, imag))):
        x = dot_nt(jnp.concatenate(pair, axis=0), basis_rows[h])
        re = x[:lines, :wide] + x[lines:, wide:]
        im = x[lines:, :wide] - x[:lines, wide:]
        pieces[0, h] = jnp.where(keep, re, 0.0).astype(BF16)
        pieces[1, h] = jnp.where(keep, im, 0.0).astype(BF16)
    rows = []
    for u in range(UNITS):
        line = [
            pieces[c, h][(2 * u + r) * GROUP:(2 * u + r + 1) * GROUP]
            for r in range(2) for c in range(2) for h in range(2)
        ]
        rows.append(jnp.concatenate(line, axis=1))
    picked = dot(jnp.concatenate(rows, axis=0), spots[...]).astype(BF16)
    return jnp.concatenate([picked[u * GROUP:(u + 1) * GROUP] for u in range(UNITS)], axis=1)


def prolong(coarse, basis_rows, spots, iterate, out_ref):
    wide = 2 * LANES
    stacked = jnp.concatenate([coarse[:, u * LANES:(u + 1) * LANES] for u in range(UNITS)], axis=0)
    spread = dot_nt(stacked, spots[...])
    spread = jnp.where(on_diagonal(spread.shape), spread, 0.0).astype(BF16)
    moved = []
    for h in range(2):
        upper, lower = [], []
        for r in range(RHS):
            u = r // 2
            first = (r % 2) * 1024 + h * wide
            re = spread[u * GROUP:(u + 1) * GROUP, first:first + wide]
            im = spread[u * GROUP:(u + 1) * GROUP, first + 512:first + 512 + wide]
            upper.append(jnp.concatenate([re, -im], axis=1))
            lower.append(jnp.concatenate([im, re], axis=1))
        moved.append(dot(jnp.concatenate(upper + lower, axis=0), basis_rows[h]))
    lines = RHS * GROUP
    real = moved[0][:lines] + pltpu.roll(moved[1][:lines], wide - 64, 1)
    imag = moved[1][lines:] + pltpu.roll(moved[0][lines:], 64, 1)
    low = iota((GROUP, LANES), 1) < 64
    for r in range(RHS):
        re, im = real[r * GROUP:(r + 1) * GROUP], imag[r * GROUP:(r + 1) * GROUP]
        tiles = (re[:, :LANES], jnp.where(low, re[:, LANES:], im[:, :LANES]), im[:, LANES:])
        for i, tile in enumerate(tiles):
            part = slice((r * 3 + i) * LANES, (r * 3 + i + 1) * LANES)
            out_ref[:, part] = (iterate[:, part].astype(F32) + tile).astype(BF16)


def coarse_kernel(
    n_ta, n_xyz, cap, block,
    residual_hbm, iterate_hbm, basis_hbm, counts_ref, links_hbm, out_ref,
    residual, iterate, basis, basis_rows, spots, vec, tiles, fin, scat, zin, zout, cnt, links, weights, lhs, part, perm, pick,
    send_a, recv_a, send_c, recv_c, send_e, recv_e, send_z, recv_z, send_n, recv_n, sem_l, sem_r, sem_i, sem_b,
):
    slab = n_xyz * block
    extent_x = slab // (LY * LZ)
    t = lax.axis_index("ta")
    o = lax.axis_index("xyz")
    up = lax.rem(t + 1, n_ta)
    down = lax.rem(t + n_ta - 1, n_ta)
    peers = [lax.rem(o + d, n_xyz) for d in range(1, n_xyz)]

    load_r = pltpu.make_async_copy(residual_hbm, residual, sem_r)
    load_r.start()
    load_b = pltpu.make_async_copy(basis_hbm, basis, sem_b)
    load_b.start()
    load = pltpu.make_async_copy(links_hbm, links, sem_l)
    load.start()
    load_i = pltpu.make_async_copy(iterate_hbm, iterate, sem_i)
    load_i.start()
    barrier = pltpu.get_barrier_semaphore()
    for peer in peers:
        pl.semaphore_signal(barrier, inc=1, device_id=(t, peer), device_id_type=MESH)
    for row in (up, down):
        pl.semaphore_signal(barrier, inc=1, device_id=(row, o), device_id_type=MESH)

    cnt[0] = jnp.zeros((8, LANES), jnp.int32)
    cnt[0, 0:1, 0:n_xyz] = counts_ref[...]
    mine = pl.ds(pl.multiple_of(o * block, block), block)
    my_tile = pl.ds(pl.multiple_of(o * cap, cap), cap)
    spot_id, spot_lane = iota((2048, LANES), 0), iota((2048, LANES), 1)
    spots[...] = one_hot(spot_lane == (spot_id >> 9) * 32 + ((spot_id >> 4) & 15) * 2 + ((spot_id >> 8) & 1))
    load_r.wait()
    load_b.wait()
    vec[mine, :] = restrict(residual, basis, basis_rows, spots)
    pl.semaphore_wait(barrier, n_xyz + 1)

    def remote(src, dst, send, recv, device):
        copy = pltpu.make_async_remote_copy(
            src_ref=src, dst_ref=dst, send_sem=send, recv_sem=recv,
            device_id=device, device_id_type=MESH,
        )
        copy.start()
        return copy

    def to_slice(src_of, dst, send, recv):
        return [
            remote(src_of(peer), dst, send.at[d], recv.at[d], (t, peer))
            for d, peer in enumerate(peers)
        ]

    copies_n = [
        remote(cnt.at[0], cnt.at[1 + side], send_n.at[side], recv_n.at[side], (row, o))
        for side, row in enumerate((down, up))
    ]
    copies_a = to_slice(lambda peer: vec.at[mine], vec.at[mine], send_a, recv_a)

    r_id, c_id = iota((512, 512), 0), iota((512, 512), 1)
    perm[...] = one_hot(c_id == ((r_id >> 5) & 3) * 128 + (r_id >> 7) * 32 + (r_id & 31))
    pick[...] = one_hot((iota((2048, LANES), 0) >> 4) == iota((2048, LANES), 1))

    counts = cnt[0, 0:1, :].astype(F32)
    lane = iota((1, LANES), 1)

    def start_of(row):
        return jnp.sum(jnp.where(lane < o, row, 0.0), axis=1, keepdims=True).astype(jnp.int32)

    start = start_of(counts)
    own_count = jnp.sum(jnp.where(lane == o, counts, 0.0), axis=1, keepdims=True).astype(jnp.int32)
    position = start + iota((cap, slab), 0)
    gather = jnp.concatenate(
        [one_hot(position == site) for site in shifted_sites(iota((cap, slab), 1), extent_x)], axis=0
    )
    slot_owner = iota((1, n_xyz * cap), 1) // cap
    slot_start = jnp.zeros((1, n_xyz * cap), jnp.int32)
    slot_count = jnp.zeros((1, n_xyz * cap), jnp.int32)
    for p in range(n_xyz):
        value = cnt[0, 0:1, p:p + 1]
        slot_start = slot_start + jnp.where(slot_owner > p, value, 0)
        slot_count = slot_count + jnp.where(slot_owner == p, value, 0)
    slot = iota((1, n_xyz * cap), 1) - slot_owner * cap
    slot_site = jnp.where(slot < slot_count, slot_start + slot, -1)
    held = one_hot(iota((slab, n_xyz * cap), 0) == slot_site)
    gather_tiles = dot(gather, held).astype(BF16)
    slot_lane = iota((slab, cap), 1)
    spread = one_hot((iota((slab, cap), 0) == start + slot_lane) & (slot_lane < own_count))

    load.wait()
    lane_q = iota((cap, LANES), 1)

    def minus_identity(q):
        place = lane_q + q * LANES
        return jnp.where((place >> 5) == (place & 31), -1.0, 0.0).astype(BF16)

    for group in range(3):
        rows = []
        for q in range(16):
            part_q = slice(q * LANES, (q + 1) * LANES)
            if group == 0:
                pieces = [links[m, :, part_q] for m in (0, 1, 2, 3)]
            elif group == 1:
                pieces = [links[m, :, part_q] for m in (4, 5, 6)] + [minus_identity(q)]
            else:
                pieces = [links[m, :, part_q] for m in (7, 8)]
            rows.append(jnp.concatenate(pieces, axis=1))
        stacked = jnp.concatenate(rows, axis=0)
        moved = dot(stacked, perm[0:stacked.shape[1], :]).astype(BF16)
        for q in range(16):
            for a in range(4):
                for g in range(2):
                    at = (q * 4 + a) * GROUP
                    first = q * cap + g * GROUP
                    weights[g, at:at + GROUP, group * LANES:(group + 1) * LANES] = moved[
                        first:first + GROUP, a * LANES:(a + 1) * LANES]

    def set_lhs(group, blocks):
        stacked = jnp.concatenate(
            [jnp.concatenate([b[:, u * LANES:(u + 1) * LANES] for b in blocks], axis=1) for u in range(UNITS)],
            axis=0,
        )
        moved = dot(stacked, perm[0:stacked.shape[1], :]).astype(BF16)
        for u in range(UNITS):
            for b in range(4):
                for g in range(2):
                    at = (u * 4 + b) * GROUP
                    first = u * cap + g * GROUP
                    lhs[g, at:at + GROUP, group * LANES:(group + 1) * LANES] = moved[
                        first:first + GROUP, b * LANES:(b + 1) * LANES]

    for copy in copies_n:
        copy.wait()
    away = []
    for side in range(2):
        row_start = start_of(cnt[1 + side, 0:1, :].astype(F32))
        away.append(one_hot(row_start + iota((cap, slab), 0) == iota((cap, slab), 1)))
    away = jnp.concatenate(away, axis=0)
    away_tiles = dot(away, held).astype(BF16)

    rhs_rows = None
    diagonal = (iota((GROUP, 512), 1) & (GROUP - 1)) == iota((GROUP, 512), 0)
    for sweep in range(SWEEPS):
        if sweep == 0:
            for copy in copies_a:
                copy.wait()
            source, near, far = vec, gather, away
        else:
            for copy in copies_c:
                copy.wait()
            source, near, far = tiles, gather_tiles, away_tiles
        full = source[...]
        zout[sweep] = dot(far, full).astype(BF16)
        copies_z = [
            remote(
                zout.at[sweep, pl.ds(side * cap, cap)], zin.at[sweep, pl.ds((1 - side) * cap, cap)],
                send_z.at[sweep, side], recv_z.at[sweep, side], (row, o),
            )
            for side, row in enumerate((up, down))
        ]
        around = dot(near, full).astype(BF16)
        blocks = [around[m * cap:(m + 1) * cap] for m in range(7)]
        if sweep == 0:
            rhs_rows = blocks[0]
        set_lhs(0, blocks[0:4])
        set_lhs(1, blocks[4:7] + [rhs_rows])
        for g in range(2):
            part[g] = dot_nt(lhs[g, :, 0:256], weights[g, :, 0:256])
        for copy in copies_z:
            copy.wait()
        set_lhs(2, [zin[sweep, 0:cap], zin[sweep, cap:2 * cap]])
        updated = []
        for g in range(2):
            total = part[g] + dot_nt(lhs[g, :, 256:384], weights[g, :, 256:384])
            rows = []
            for u in range(UNITS):
                pieces = []
                for r in range(2):
                    at = (u * 4 + r * 2) * GROUP
                    from_real, from_imag = total[at:at + GROUP], total[at + GROUP:at + 2 * GROUP]
                    real = from_imag[:, 512:] - from_real[:, :512]
                    imag = -(from_real[:, 512:] + from_imag[:, :512])
                    pieces += [jnp.where(diagonal, v, 0.0).astype(BF16) for v in (real, imag)]
                rows.append(jnp.concatenate(pieces, axis=1))
            picked = dot(jnp.concatenate(rows, axis=0), pick[...]).astype(BF16)
            updated.append(jnp.concatenate([picked[u * GROUP:(u + 1) * GROUP] for u in range(UNITS)], axis=1))
        tile = jnp.concatenate(updated, axis=0)
        if sweep < SWEEPS - 1:
            tiles[my_tile, :] = tile
            copies_c = to_slice(lambda peer: tiles.at[my_tile], tiles.at[my_tile], send_c, recv_c)
    scat[...] = dot(spread, tile).astype(BF16)
    copies_e = to_slice(
        lambda peer: scat.at[pl.ds(pl.multiple_of(peer * block, block), block)], fin.at[o], send_e, recv_e
    )
    fin[o] = scat[mine, :]
    for copy in copies_e:
        copy.wait()
    total = fin[0].astype(F32)
    for p in range(1, n_xyz):
        total = total + fin[p].astype(F32)
    load_i.wait()
    prolong(total.astype(BF16), basis_rows, spots, iterate, out_ref)


def on_device(n_ta, n_xyz, residual, iterate, prolongator, coarse_links, owner_counts):
    block = residual.shape[0]
    cap = coarse_links.shape[1]
    slab = n_xyz * block
    vmem = pl.BlockSpec(memory_space=pltpu.VMEM)
    hbm = pl.BlockSpec(memory_space=pl.ANY)
    dma = pltpu.SemaphoreType.DMA
    return pl.pallas_call(
        functools.partial(coarse_kernel, n_ta, n_xyz, cap, block),
        out_shape=jax.ShapeDtypeStruct(residual.shape, BF16),
        in_specs=[hbm, hbm, hbm, vmem, hbm],
        out_specs=vmem,
        scratch_shapes=[
            pltpu.VMEM(residual.shape, BF16),
            pltpu.VMEM(iterate.shape, BF16),
            pltpu.VMEM(prolongator.shape, BF16),
            pltpu.VMEM((2, NV * GROUP, 2 * LANES), BF16),
            pltpu.VMEM((2048, LANES), BF16),
            pltpu.VMEM((slab, COLS), BF16),
            pltpu.VMEM((n_xyz * cap, COLS), BF16),
            pltpu.VMEM((n_xyz, block, COLS), BF16),
            pltpu.VMEM((slab, COLS), BF16),
            pltpu.VMEM((SWEEPS, 2 * cap, COLS), BF16),
            pltpu.VMEM((SWEEPS, 2 * cap, COLS), BF16),
            pltpu.VMEM((3, 8, LANES), jnp.int32),
            pltpu.VMEM(coarse_links.shape, BF16),
            pltpu.VMEM((2, 64 * GROUP, 3 * LANES), BF16),
            pltpu.VMEM((2, 24 * GROUP, 3 * LANES), BF16),
            pltpu.VMEM((2, 24 * GROUP, 64 * GROUP), F32),
            pltpu.VMEM((512, 512), BF16),
            pltpu.VMEM((2048, LANES), BF16),
            dma((n_xyz - 1,)), dma((n_xyz - 1,)),
            dma((n_xyz - 1,)), dma((n_xyz - 1,)),
            dma((n_xyz - 1,)), dma((n_xyz - 1,)),
            dma((SWEEPS, 2)), dma((SWEEPS, 2)),
            dma((2,)), dma((2,)),
            dma, dma, dma, dma,
        ],
        compiler_params=pltpu.CompilerParams(
            collective_id=0, has_side_effects=True, vmem_limit_bytes=60 * 1024 * 1024
        ),
    )(residual, iterate, prolongator, owner_counts, coarse_links)


def solution(mesh):
    in_specs = (
        P(("ta", "xyz"), None),
        P(("ta", "xyz"), None),
        P(("ta", "xyz"), None),
        P(None, ("ta", "xyz"), None),
        P("ta", None),
    )
    out_specs = P(("ta", "xyz"), None)
    return jax.shard_map(
        functools.partial(on_device, mesh.shape["ta"], mesh.shape["xyz"]),
        mesh=mesh, in_specs=in_specs, out_specs=out_specs, check_vma=False,
    )
```

```python
import functools

import jax
import jax.numpy as jnp
from jax import lax
from jax.experimental import pallas as pl
from jax.experimental.pallas import tpu as pltpu
from jax.sharding import PartitionSpec as P

NV = 32
FB = 192
RHS = 12
LY = 2
LZ = 8
SWEEPS = 2
COLS = RHS * 2 * NV
LANES = 128
UNITS = COLS // LANES
GROUP = 16
MESH = pl.DeviceIdType.MESH
F32 = jnp.float32
BF16 = jnp.bfloat16


def iota(shape, dim):
    return lax.broadcasted_iota(jnp.int32, shape, dim)


def dot(left, right):
    return jnp.dot(left, right, preferred_element_type=F32)


def dot_nt(left, right):
    return lax.dot_general(left, right, (((1,), (1,)), ((), ())), preferred_element_type=F32)


def one_hot(condition):
    return jnp.where(condition, 1.0, 0.0).astype(BF16)


def shifted_sites(site, extent_x):
    bits_x = extent_x.bit_length() - 1
    x = site & (extent_x - 1)
    z = (site >> bits_x) & (LZ - 1)
    y = site >> (bits_x + 3)

    def site_of(ax, ay, az):
        return ((((ay & (LY - 1)) << 3) + (az & (LZ - 1))) << bits_x) + (ax & (extent_x - 1))

    return [
        site,
        site_of(x - 1, y, z),
        site_of(x + 1, y, z),
        site_of(x, y - 1, z),
        site_of(x, y + 1, z),
        site_of(x, y, z - 1),
        site_of(x, y, z + 1),
    ]


def on_diagonal(shape):
    return (iota(shape, 1) & (GROUP - 1)) == (iota(shape, 0) & (GROUP - 1))


def restrict(residual, basis, basis_rows, spots):
    wide = 2 * LANES
    lane = iota((GROUP, wide), 1)
    for h in range(2):
        for pair in range(NV):
            first = pair * 2 * FB + h * LANES
            basis_rows[h, pair * GROUP:(pair + 1) * GROUP, :] = basis[:, first:first + wide]
    real, imag = [], []
    for r in range(RHS):
        first = r * 2 * FB
        real.append(jnp.where(lane < FB, residual[:, first:first + wide], 0.0).astype(BF16))
        imag.append(jnp.where(lane >= wide - FB, residual[:, first + LANES:first + LANES + wide], 0.0).astype(BF16))
    real, imag = jnp.concatenate(real, axis=0), jnp.concatenate(imag, axis=0)
    row_id, col_id = iota((wide, wide), 0), iota((wide, wide), 1)
    real_late = dot(real, one_hot(col_id == row_id + 64)).astype(BF16)
    imag_early = dot(imag, one_hot(col_id == row_id - 64)).astype(BF16)
    lines = RHS * GROUP
    keep = on_diagonal((lines, wide))
    pieces = {}
    for h, pair in enumerate(((real, imag_early), (real_late, imag))):
        x = dot_nt(jnp.concatenate(pair, axis=0), basis_rows[h])
        re = x[:lines, :wide] + x[lines:, wide:]
        im = x[lines:, :wide] - x[:lines, wide:]
        pieces[0, h] = jnp.where(keep, re, 0.0).astype(BF16)
        pieces[1, h] = jnp.where(keep, im, 0.0).astype(BF16)
    rows = []
    for u in range(UNITS):
        line = [
            pieces[c, h][(2 * u + r) * GROUP:(2 * u + r + 1) * GROUP]
            for r in range(2) for c in range(2) for h in range(2)
        ]
        rows.append(jnp.concatenate(line, axis=1))
    picked = dot(jnp.concatenate(rows, axis=0), spots[...]).astype(BF16)
    return jnp.concatenate([picked[u * GROUP:(u + 1) * GROUP] for u in range(UNITS)], axis=1)


def prolong(coarse, basis_rows, spots, iterate, out_ref):
    wide = 2 * LANES
    stacked = jnp.concatenate([coarse[:, u * LANES:(u + 1) * LANES] for u in range(UNITS)], axis=0)
    spread = dot_nt(stacked, spots[...])
    spread = jnp.where(on_diagonal(spread.shape), spread, 0.0).astype(BF16)
    moved = []
    for h in range(2):
        upper, lower = [], []
        for r in range(RHS):
            u = r // 2
            first = (r % 2) * 1024 + h * wide
            re = spread[u * GROUP:(u + 1) * GROUP, first:first + wide]
            im = spread[u * GROUP:(u + 1) * GROUP, first + 512:first + 512 + wide]
            upper.append(jnp.concatenate([re, -im], axis=1))
            lower.append(jnp.concatenate([im, re], axis=1))
        moved.append(dot(jnp.concatenate(upper + lower, axis=0), basis_rows[h]))
    lines = RHS * GROUP
    real = moved[0][:lines] + pltpu.roll(moved[1][:lines], wide - 64, 1)
    imag = moved[1][lines:] + pltpu.roll(moved[0][lines:], 64, 1)
    low = iota((GROUP, LANES), 1) < 64
    for r in range(RHS):
        re, im = real[r * GROUP:(r + 1) * GROUP], imag[r * GROUP:(r + 1) * GROUP]
        tiles = (re[:, :LANES], jnp.where(low, re[:, LANES:], im[:, :LANES]), im[:, LANES:])
        for i, tile in enumerate(tiles):
            part = slice((r * 3 + i) * LANES, (r * 3 + i + 1) * LANES)
            out_ref[:, part] = iterate[:, part].astype(F32) + tile


def coarse_kernel(
    n_ta, n_xyz, cap, block,
    residual_hbm, iterate_hbm, basis_hbm, counts_ref, links_hbm, out_ref,
    residual, iterate, basis, basis_rows, spots, vec, tiles, fin, scat, zin, zout, cnt, links, weights, lhs, part, perm, pick,
    send_a, recv_a, send_c, recv_c, send_e, recv_e, send_z, recv_z, send_n, recv_n, sem_l, sem_r, sem_i, sem_b,
):
    slab = n_xyz * block
    extent_x = slab // (LY * LZ)
    t = lax.axis_index("ta")
    o = lax.axis_index("xyz")
    up = lax.rem(t + 1, n_ta)
    down = lax.rem(t + n_ta - 1, n_ta)
    peers = [lax.rem(o + d, n_xyz) for d in range(1, n_xyz)]

    load_r = pltpu.make_async_copy(residual_hbm, residual, sem_r)
    load_r.start()
    load_b = pltpu.make_async_copy(basis_hbm, basis, sem_b)
    load_b.start()
    load = pltpu.make_async_copy(links_hbm, links, sem_l)
    load.start()
    load_i = pltpu.make_async_copy(iterate_hbm, iterate, sem_i)
    load_i.start()
    barrier = pltpu.get_barrier_semaphore()
    for peer in peers:
        pl.semaphore_signal(barrier, inc=1, device_id=(t, peer), device_id_type=MESH)
    for row in (up, down):
        pl.semaphore_signal(barrier, inc=1, device_id=(row, o), device_id_type=MESH)

    cnt[0] = jnp.zeros((8, LANES), jnp.int32)
    cnt[0, 0:1, 0:n_xyz] = counts_ref[...]
    mine = pl.ds(pl.multiple_of(o * block, block), block)
    my_tile = pl.ds(pl.multiple_of(o * cap, cap), cap)
    spot_id, spot_lane = iota((2048, LANES), 0), iota((2048, LANES), 1)
    spots[...] = one_hot(spot_lane == (spot_id >> 9) * 32 + ((spot_id >> 4) & 15) * 2 + ((spot_id >> 8) & 1))
    load_r.wait()
    load_b.wait()
    vec[mine, :] = restrict(residual, basis, basis_rows, spots)
    pl.semaphore_wait(barrier, n_xyz + 1)

    def remote(src, dst, send, recv, device):
        copy = pltpu.make_async_remote_copy(
            src_ref=src, dst_ref=dst, send_sem=send, recv_sem=recv,
            device_id=device, device_id_type=MESH,
        )
        copy.start()
        return copy

    def to_slice(src_of, dst, send, recv):
        return [
            remote(src_of(peer), dst, send.at[d], recv.at[d], (t, peer))
            for d, peer in enumerate(peers)
        ]

    copies_n = [
        remote(cnt.at[0], cnt.at[1 + side], send_n.at[side], recv_n.at[side], (row, o))
        for side, row in enumerate((down, up))
    ]
    copies_a = to_slice(lambda peer: vec.at[mine], vec.at[mine], send_a, recv_a)

    r_id, c_id = iota((512, 512), 0), iota((512, 512), 1)
    perm[...] = one_hot(c_id == ((r_id >> 5) & 3) * 128 + (r_id >> 7) * 32 + (r_id & 31))
    pick[...] = one_hot((iota((2048, LANES), 0) >> 4) == iota((2048, LANES), 1))

    counts = cnt[0, 0:1, :].astype(F32)
    lane = iota((1, LANES), 1)

    def start_of(row):
        return jnp.sum(jnp.where(lane < o, row, 0.0), axis=1, keepdims=True).astype(jnp.int32)

    start = start_of(counts)
    own_count = jnp.sum(jnp.where(lane == o, counts, 0.0), axis=1, keepdims=True).astype(jnp.int32)
    position = start + iota((cap, slab), 0)
    gather = jnp.concatenate(
        [one_hot(position == site) for site in shifted_sites(iota((cap, slab), 1), extent_x)], axis=0
    )
    slot_owner = iota((1, n_xyz * cap), 1) // cap
    slot_start = jnp.zeros((1, n_xyz * cap), jnp.int32)
    slot_count = jnp.zeros((1, n_xyz * cap), jnp.int32)
    for p in range(n_xyz):
        value = cnt[0, 0:1, p:p + 1]
        slot_start = slot_start + jnp.where(slot_owner > p, value, 0)
        slot_count = slot_count + jnp.where(slot_owner == p, value, 0)
    slot = iota((1, n_xyz * cap), 1) - slot_owner * cap
    slot_site = jnp.where(slot < slot_count, slot_start + slot, -1)
    held = one_hot(iota((slab, n_xyz * cap), 0) == slot_site)
    gather_tiles = dot(gather, held).astype(BF16)
    slot_lane = iota((slab, cap), 1)
    spread = one_hot((iota((slab, cap), 0) == start + slot_lane) & (slot_lane < own_count))

    load.wait()
    lane_q = iota((cap, LANES), 1)

    def minus_identity(q):
        place = lane_q + q * LANES
        return jnp.where((place >> 5) == (place & 31), -1.0, 0.0).astype(BF16)

    for group in range(3):
        rows = []
        for q in range(16):
            part_q = slice(q * LANES, (q + 1) * LANES)
            if group == 0:
                pieces = [links[m, :, part_q] for m in (0, 1, 2, 3)]
            elif group == 1:
                pieces = [links[m, :, part_q] for m in (4, 5, 6)] + [minus_identity(q)]
            else:
                pieces = [links[m, :, part_q] for m in (7, 8)]
            rows.append(jnp.concatenate(pieces, axis=1))
        stacked = jnp.concatenate(rows, axis=0)
        moved = dot(stacked, perm[0:stacked.shape[1], :]).astype(BF16)
        for q in range(16):
            for a in range(4):
                for g in range(2):
                    at = (q * 4 + a) * GROUP
                    first = q * cap + g * GROUP
                    weights[g, at:at + GROUP, group * LANES:(group + 1) * LANES] = moved[
                        first:first + GROUP, a * LANES:(a + 1) * LANES]

    def set_lhs(group, blocks):
        stacked = jnp.concatenate(
            [jnp.concatenate([b[:, u * LANES:(u + 1) * LANES] for b in blocks], axis=1) for u in range(UNITS)],
            axis=0,
        )
        moved = dot(stacked, perm[0:stacked.shape[1], :]).astype(BF16)
        for u in range(UNITS):
            for b in range(4):
                for g in range(2):
                    at = (u * 4 + b) * GROUP
                    first = u * cap + g * GROUP
                    lhs[g, at:at + GROUP, group * LANES:(group + 1) * LANES] = moved[
                        first:first + GROUP, b * LANES:(b + 1) * LANES]

    for copy in copies_n:
        copy.wait()
    away = []
    for side in range(2):
        row_start = start_of(cnt[1 + side, 0:1, :].astype(F32))
        away.append(one_hot(row_start + iota((cap, slab), 0) == iota((cap, slab), 1)))
    away = jnp.concatenate(away, axis=0)
    away_tiles = dot(away, held).astype(BF16)

    rhs_rows = None
    diagonal = (iota((GROUP, 512), 1) & (GROUP - 1)) == iota((GROUP, 512), 0)
    for sweep in range(SWEEPS):
        if sweep == 0:
            for copy in copies_a:
                copy.wait()
            source, near, far = vec, gather, away
        else:
            for copy in copies_c:
                copy.wait()
            source, near, far = tiles, gather_tiles, away_tiles
        full = source[...]
        zout[sweep] = dot(far, full).astype(BF16)
        copies_z = [
            remote(
                zout.at[sweep, pl.ds(side * cap, cap)], zin.at[sweep, pl.ds((1 - side) * cap, cap)],
                send_z.at[sweep, side], recv_z.at[sweep, side], (row, o),
            )
            for side, row in enumerate((up, down))
        ]
        around = dot(near, full).astype(BF16)
        blocks = [around[m * cap:(m + 1) * cap] for m in range(7)]
        if sweep == 0:
            rhs_rows = blocks[0]
        set_lhs(0, blocks[0:4])
        set_lhs(1, blocks[4:7] + [rhs_rows])
        for g in range(2):
            part[g] = dot_nt(lhs[g, :, 0:256], weights[g, :, 0:256])
        for copy in copies_z:
            copy.wait()
        set_lhs(2, [zin[sweep, 0:cap], zin[sweep, cap:2 * cap]])
        updated = []
        for g in range(2):
            total = part[g] + dot_nt(lhs[g, :, 256:384], weights[g, :, 256:384])
            rows = []
            for u in range(UNITS):
                pieces = []
                for r in range(2):
                    at = (u * 4 + r * 2) * GROUP
                    from_real, from_imag = total[at:at + GROUP], total[at + GROUP:at + 2 * GROUP]
                    real = from_imag[:, 512:] - from_real[:, :512]
                    imag = -(from_real[:, 512:] + from_imag[:, :512])
                    pieces += [jnp.where(diagonal, v, 0.0).astype(BF16) for v in (real, imag)]
                rows.append(jnp.concatenate(pieces, axis=1))
            picked = dot(jnp.concatenate(rows, axis=0), pick[...]).astype(BF16)
            updated.append(jnp.concatenate([picked[u * GROUP:(u + 1) * GROUP] for u in range(UNITS)], axis=1))
        tile = jnp.concatenate(updated, axis=0)
        if sweep < SWEEPS - 1:
            tiles[my_tile, :] = tile
            copies_c = to_slice(lambda peer: tiles.at[my_tile], tiles.at[my_tile], send_c, recv_c)
    scat[...] = dot(spread, tile).astype(BF16)
    copies_e = to_slice(
        lambda peer: scat.at[pl.ds(pl.multiple_of(peer * block, block), block)], fin.at[o], send_e, recv_e
    )
    fin[o] = scat[mine, :]
    for copy in copies_e:
        copy.wait()
    total = fin[0].astype(F32)
    for p in range(1, n_xyz):
        total = total + fin[p].astype(F32)
    load_i.wait()
    prolong(total.astype(BF16), basis_rows, spots, iterate, out_ref)


def on_device(n_ta, n_xyz, residual, iterate, prolongator, coarse_links, owner_counts):
    block = residual.shape[0]
    cap = coarse_links.shape[1]
    slab = n_xyz * block
    vmem = pl.BlockSpec(memory_space=pltpu.VMEM)
    hbm = pl.BlockSpec(memory_space=pl.ANY)
    dma = pltpu.SemaphoreType.DMA
    summed = pl.pallas_call(
        functools.partial(coarse_kernel, n_ta, n_xyz, cap, block),
        out_shape=jax.ShapeDtypeStruct(residual.shape, F32),
        in_specs=[hbm, hbm, hbm, vmem, hbm],
        out_specs=vmem,
        scratch_shapes=[
            pltpu.VMEM(residual.shape, BF16),
            pltpu.VMEM(iterate.shape, BF16),
            pltpu.VMEM(prolongator.shape, BF16),
            pltpu.VMEM((2, NV * GROUP, 2 * LANES), BF16),
            pltpu.VMEM((2048, LANES), BF16),
            pltpu.VMEM((slab, COLS), BF16),
            pltpu.VMEM((n_xyz * cap, COLS), BF16),
            pltpu.VMEM((n_xyz, block, COLS), BF16),
            pltpu.VMEM((slab, COLS), BF16),
            pltpu.VMEM((SWEEPS, 2 * cap, COLS), BF16),
            pltpu.VMEM((SWEEPS, 2 * cap, COLS), BF16),
            pltpu.VMEM((3, 8, LANES), jnp.int32),
            pltpu.VMEM(coarse_links.shape, BF16),
            pltpu.VMEM((2, 64 * GROUP, 3 * LANES), BF16),
            pltpu.VMEM((2, 24 * GROUP, 3 * LANES), BF16),
            pltpu.VMEM((2, 24 * GROUP, 64 * GROUP), F32),
            pltpu.VMEM((512, 512), BF16),
            pltpu.VMEM((2048, LANES), BF16),
            dma((n_xyz - 1,)), dma((n_xyz - 1,)),
            dma((n_xyz - 1,)), dma((n_xyz - 1,)),
            dma((n_xyz - 1,)), dma((n_xyz - 1,)),
            dma((SWEEPS, 2)), dma((SWEEPS, 2)),
            dma((2,)), dma((2,)),
            dma, dma, dma, dma,
        ],
        compiler_params=pltpu.CompilerParams(
            collective_id=0, has_side_effects=True, vmem_limit_bytes=60 * 1024 * 1024
        ),
    )(residual, iterate, prolongator, owner_counts, coarse_links)
    return summed.astype(BF16)


def solution(mesh):
    in_specs = (
        P(("ta", "xyz"), None),
        P(("ta", "xyz"), None),
        P(("ta", "xyz"), None),
        P(None, ("ta", "xyz"), None),
        P("ta", None),
    )
    out_specs = P(("ta", "xyz"), None)
    return jax.shard_map(
        functools.partial(on_device, mesh.shape["ta"], mesh.shape["xyz"]),
        mesh=mesh, in_specs=in_specs, out_specs=out_specs, check_vma=False,
    )
```
